32 devices in a mesh: parts: 2 (over y), fsdp: 4 (over z), tok: 4 (over x, core).
Axes of the slice: x: 2, y: 2, z: 4, core: 2. Of those that a mesh axis runs over, the one named last changes fastest.
Arguments:
- tokens: bfloat16 [64, 6144], P(('parts', 'fsdp', 'tok')), parts along dimension 0, may hold values from -6 to 6
- route_logits: bfloat16 [64, 2], P(('parts', 'fsdp', 'tok')), parts along dimension 0, may hold values from -6 to 6
- expert_ids: int32 [64, 2], P(('parts', 'fsdp', 'tok')), parts along dimension 0, may hold values from 0 to 7, all different within a row
- gate_weight: bfloat16 [6144, 16384], P('tok', 'fsdp'), may hold values from -0.078125 to 0.078125
- up_weight: bfloat16 [6144, 16384], P('tok', 'fsdp'), may hold values from -0.078125 to 0.078125
- down_weight: bfloat16 [16384, 6144], P(('fsdp', 'tok')), may hold values from -0.046875 to 0.046875
- a_factors: bfloat16 [8, 512, 6144], P(None, 'fsdp'), may hold values from -0.078125 to 0.078125
- b_factors: bfloat16 [8, 2, 256, 16384], P(None, None, 'tok', 'fsdp'), may hold values from -0.25 to 0.25
Outputs:
- mixed: bfloat16 [64, 6144], P(('parts', 'fsdp', 'tok')), parts along dimension 0
The draws below stay inside these ranges and needn't reach their ends.
There are 2 independent parts, one for each index of `parts`. The reference program is written for one: setup_inputs(seed, part) draws one part's arguments, and reference() takes and returns one part's arrays. A program takes and returns all parts, laid end to end along the dimension named above; an argument that names none is the same for every part. Nothing has to cross between parts.
Inputs may be any that keep to these rules, and one draw needn't show every extreme that they name: `expert_ids`: every row names 2 different experts.
All inputs are finite; a program needn't handle non-finite values.
Results may differ from the reference program's by a relative error of at most 0.0055.
Values may be sent and summed in bfloat16 or wider, within the bound.
A program may use at most 512 MiB of HBM per device.

```python
import jax
import jax.numpy as jnp
from jax import lax

D = 6144
FF = 16384
EXPERTS = 8
TOPK = 2
RANK = 256
TOKENS = 32


def level_of(key, shape, shards, low, top_value):
    level, own = 1.0, jax.random.fold_in(key, 6)
    for position, shards_of in shards:
        heights = jnp.exp(jax.random.uniform(jax.random.fold_in(own, position), (shards_of,), jnp.float32, low / len(shards), top_value / len(shards)))
        level = level * jnp.repeat(heights, shape[position] // shards_of).reshape([-1 if axis == position else 1 for axis in range(len(shape))])
    return level


def distinct(rng, rows, amount, top, lift):
    ranking = jax.random.permutation(jax.random.fold_in(rng, 1), amount)
    pull = ranking
    for power in range(3):
        pull = pull * pull // amount
    pull = pull * lift // amount
    chance = jax.random.randint(jax.random.fold_in(rng, 2), (rows, amount), 0, 4096) + pull
    holders = jax.random.permutation(jax.random.fold_in(rng, 3), rows)[jnp.arange(amount) % rows]
    chance = jnp.where(jnp.arange(rows)[:, None] == holders[None, :], 1 << 14, chance)
    score = chance * amount + jnp.arange(amount)
    return lax.top_k(score.astype(jnp.int32), top)[1].astype(jnp.int32)


def scatter_about(key, shape, scale, limit, cuts=(), held_as=jnp.bfloat16):
    factor_of = level_of(key, shape, cuts, -0.22, 0.18) if cuts else 1.0
    result = jax.random.normal(key, shape, jnp.float32) * scale * factor_of
    return jnp.minimum(jnp.maximum(result, -limit), limit).astype(held_as)


def setup_inputs(seed: int = 0, part: int = 0) -> dict:
    keys = jax.random.split(jax.random.key(seed), 9)
    part_splits = jax.random.split(jax.random.fold_in(keys[8], part), 9)
    return {
        "tokens": scatter_about(part_splits[0], (TOKENS, D), 1.0, 6.0, ((0, 16),)),
        "route_logits": scatter_about(part_splits[1], (TOKENS, TOPK), 1.5, 6.0, ((0, 16),)),
        "expert_ids": distinct(part_splits[2], TOKENS, EXPERTS, TOPK, 4096),
        "gate_weight": scatter_about(keys[3], (D, FF), D ** -0.5, 0.078125, ((0, 4), (1, 4))),
        "up_weight": scatter_about(keys[4], (D, FF), D ** -0.5, 0.078125, ((0, 4), (1, 4))),
        "down_weight": scatter_about(keys[5], (FF, D), FF ** -0.5, 0.046875, ((0, 16),)),
        "a_factors": scatter_about(keys[6], (EXPERTS, 2 * RANK, D), D ** -0.5, 0.078125, ((1, 4),)),
        "b_factors": scatter_about(keys[7], (EXPERTS, 2, RANK, FF), (2 * RANK) ** -0.5, 0.25, ((2, 4), (3, 4))),
    }


def mix_hidden(base_gate, base_up, logit_rows, selector, codes, low_cols):
    experts = low_cols.shape[0]
    rank = low_cols.shape[2]
    width = low_cols.shape[3]
    count = base_gate.shape[0]
    topk = codes.shape[1]
    spread = selector[:, :, :, None] * codes[:, :, None, :]
    gate_codes = spread[:, :, :, :rank].reshape(count * topk, experts * rank)
    up_codes = spread[:, :, :, rank:].reshape(count * topk, experts * rank)
    delta_gate = jnp.dot(gate_codes, low_cols[:, 0].reshape(experts * rank, width), preferred_element_type=jnp.float32)
    delta_up = jnp.dot(up_codes, low_cols[:, 1].reshape(experts * rank, width), preferred_element_type=jnp.float32)
    gate = base_gate[:, None, :] + delta_gate.reshape(count, topk, width)
    upper = base_up[:, None, :] + delta_up.reshape(count, topk, width)
    scores = logit_rows.astype(jnp.float32)
    first = jax.nn.sigmoid(scores[:, 0] - scores[:, 1])
    mixing = jnp.stack([first, 1.0 - first], axis=1)
    return jnp.sum(mixing[:, :, None] * jax.nn.silu(gate) * upper, axis=1).astype(jnp.bfloat16)


def reference(tokens, route_logits, expert_ids, gate_weight, up_weight, down_weight, a_factors, b_factors):
    labels = jnp.arange(EXPERTS, dtype=jnp.int32)
    selector = (expert_ids[:, :, None] == labels[None, None, :]).astype(jnp.bfloat16)
    partial_value = jnp.einsum("rd,ejd->rej", tokens.astype(jnp.float32), a_factors.astype(jnp.float32)).astype(jnp.bfloat16)
    codes = jnp.einsum("rke,rej->rkj", selector.astype(jnp.float32), partial_value.astype(jnp.float32)).astype(jnp.bfloat16)
    base_gate = jnp.dot(tokens, gate_weight, preferred_element_type=jnp.float32)
    base_up = jnp.dot(tokens, up_weight, preferred_element_type=jnp.float32)
    hidden = mix_hidden(base_gate, base_up, route_logits, selector, codes, b_factors)
    return jnp.dot(hidden, down_weight, preferred_element_type=jnp.float32).astype(jnp.bfloat16)
```

```python
import jax
import jax.numpy as jnp
from jax import lax
from jax.sharding import PartitionSpec as P

BOTH = ("fsdp", "tok")


def per_device(
    tokens, route_logits, expert_ids, gate_weight, up_weight, down_weight, a_factors, b_factors
):
    tok_size = lax.axis_size("tok")
    tok_at = lax.axis_index("tok")
    experts, own_ranks, _ = a_factors.shape
    depth, width = gate_weight.shape
    cut = b_factors.shape[2]
    rank = cut * tok_size
    share = experts // tok_size

    token_here = lax.all_gather(tokens, BOTH, axis=0, tiled=True)
    logit_here = lax.all_gather(route_logits, BOTH, axis=0, tiled=True)
    ident_here = lax.all_gather(expert_ids, BOTH, axis=0, tiled=True)
    count, topk = ident_here.shape

    a_here = lax.dynamic_slice_in_dim(a_factors, tok_at * share, share, axis=0)
    partial_codes = jnp.einsum(
        "rd,ejd->erj", token_here, a_here, preferred_element_type=jnp.float32
    ).astype(jnp.bfloat16)
    whole_codes = lax.all_gather(partial_codes, "tok", axis=0, tiled=True)
    whole_codes = lax.all_gather(whole_codes, "fsdp", axis=2, tiled=True)

    token_part = lax.dynamic_slice_in_dim(token_here, tok_at * depth, depth, axis=1)
    base_gate = jnp.dot(token_part, gate_weight, preferred_element_type=jnp.float32)
    base_up = jnp.dot(token_part, up_weight, preferred_element_type=jnp.float32)
    chosen = ident_here.T[:, :, None] == jnp.arange(experts, dtype=jnp.int32)

    def delta(which):
        codes = lax.dynamic_slice_in_dim(whole_codes, which * rank + tok_at * cut, cut, axis=2)
        spread = jnp.where(chosen[:, :, :, None], codes.transpose(1, 0, 2)[None], 0)
        return jnp.dot(
            spread.reshape(topk * count, experts * cut),
            b_factors[:, which].reshape(experts * cut, width),
            preferred_element_type=jnp.float32,
        ).reshape(topk, count, width)

    both = jnp.stack([base_gate + delta(0), base_up + delta(1)])
    both = lax.psum_scatter(both, "tok", scatter_dimension=3, tiled=True)
    scores = logit_here.astype(jnp.float32)
    first = jax.nn.sigmoid(scores[:, 0] - scores[:, 1])
    mixing = jnp.stack([first, 1.0 - first], axis=0)
    hidden = jnp.sum(mixing[:, :, None] * jax.nn.silu(both[0]) * both[1], axis=0)
    summed = jnp.dot(
        hidden.astype(jnp.bfloat16), down_weight, preferred_element_type=jnp.float32
    )
    return lax.psum_scatter(summed, BOTH, scatter_dimension=0, tiled=True).astype(jnp.bfloat16)


def solution(mesh):
    placed = (
        P(("parts", "fsdp", "tok"), None),
        P(("parts", "fsdp", "tok"), None),
        P(("parts", "fsdp", "tok"), None),
        P("tok", "fsdp"),
        P("tok", "fsdp"),
        P(("fsdp", "tok"), None),
        P(None, "fsdp", None),
        P(None, None, "tok", "fsdp"),
    )
    return jax.shard_map(
        per_device,
        mesh=mesh,
        in_specs=placed,
        out_specs=P(("parts", "fsdp", "tok"), None),
        check_vma=False,
    )
```

```python
import jax
import jax.numpy as jnp
from jax import lax
from jax.experimental import pallas as pl
from jax.experimental.pallas import tpu as pltpu
from jax.sharding import PartitionSpec as P

BOTH = ("fsdp", "tok")
MESH = pl.DeviceIdType.MESH
F32, BF16 = jnp.float32, jnp.bfloat16
EXTRA = 128


def one_hot_rows(rows, source_of):
    row = lax.broadcasted_iota(jnp.int32, (rows, rows), 0)
    column = lax.broadcasted_iota(jnp.int32, (rows, rows), 1)
    return jnp.where(column == source_of(row), 1.0, 0.0).astype(BF16)


def dot(left, right):
    return jnp.dot(left, right, preferred_element_type=F32)


def layer_kernel(
    pack, wg_hbm, wu_hbm, wd_hbm, a_hbm, b_hbm, out,
    wg, wu, wd, av, bv, held, y_all, y_own, extra, code_send, code_slot, spread,
    base, far_sum, near_sum, near_send, far_send, x_send, near_got, far_got, x_got,
    summed, down_got, row_send, row_got, z_send, z_got,
    load_sem, tok_send_sem, tok_recv_sem, code_send_sem, code_recv_sem,
    part_send_sem, part_recv_sem, down_send_sem, down_recv_sem,
):
    f, t = lax.axis_index("fsdp"), lax.axis_index("tok")
    core_peer, x_peer, cross = (5 - t) % 4, (t + 2) % 4, 3 - t
    x_at = t // 2
    piece = pack.shape[1] - EXTRA
    depth, chunk = wg.shape[1], wg.shape[2]
    cut = b_hbm.shape[2]
    count = y_own.shape[0]
    order = (cross, x_peer, core_peer, t)

    def columns(j):
        return pl.ds(pl.multiple_of(order[j] * chunk, chunk), chunk)

    def load(index, source, target):
        return pltpu.make_async_copy(source, target, load_sem.at[index])

    def remote(source, target, send, recv, to_f, to_t):
        return pltpu.make_async_remote_copy(
            src_ref=source, dst_ref=target, send_sem=send, recv_sem=recv,
            device_id={"fsdp": to_f, "tok": to_t}, device_id_type=MESH,
        )

    a_loads = [
        load(2 * h + e, a_hbm.at[2 * t + e, pl.ds(h * cut, cut)], av.at[h, e])
        for h in range(2) for e in range(2)
    ]
    g_loads = [load(4 + j, wg_hbm.at[:, columns(j)], wg.at[j]) for j in range(4)]
    u_loads = [load(8 + j, wu_hbm.at[:, columns(j)], wu.at[j]) for j in range(4)]
    b_loads = [load(12 + j, b_hbm.at[:, :, :, columns(j)], bv.at[j]) for j in range(4)]
    d_load = load(16, wd_hbm, wd)
    for copy in a_loads + [g_loads[0], u_loads[0], g_loads[1], u_loads[1], b_loads[0], b_loads[1]]:
        copy.start()

    barrier = pltpu.get_barrier_semaphore()
    me = f * 4 + t
    for step in range(1, 16):
        other = (me + step) % 16
        pl.semaphore_signal(
            barrier, inc=1, device_id={"fsdp": other // 4, "tok": other % 4}, device_id_type=MESH
        )
    pl.semaphore_wait(barrier, 15)

    held[t, f] = pack[...]
    sends = []
    for step in range(1, 4):
        copy = remote(
            pack, held.at[t, f], tok_send_sem.at[step], tok_recv_sem.at[step], (f + step) % 4, t
        )
        copy.start()
        sends.append(copy)
    for copy in sends:
        copy.wait_recv()
    to_core = remote(held.at[t], held.at[t], tok_send_sem.at[4], tok_recv_sem.at[4], f, core_peer)
    to_x = remote(held.at[t], held.at[t], tok_send_sem.at[5], tok_recv_sem.at[5], f, x_peer)
    to_x.start()
    to_core.start()
    to_x.wait_recv()
    onward = remote(
        held.at[x_peer], held.at[x_peer], tok_send_sem.at[6], tok_recv_sem.at[6], f, core_peer
    )
    onward.start()
    sends += [to_core, to_x, onward]
    to_core.wait_recv()
    onward.wait_recv()
    for copy in [g_loads[2], u_loads[2], b_loads[2], g_loads[3], u_loads[3], b_loads[3], d_load]:
        copy.start()

    order_in = one_hot_rows(
        8 * count, lambda r: ((r & 31) >> 1) * 16 + (r & 1) * 8 + (r >> 5)
    )
    turned = dot(order_in, held[...].reshape(8 * count, piece + EXTRA))
    y_all[...] = turned[:, :piece].astype(BF16)
    extra[...] = turned[:count, piece:]
    for half in range(2):
        rows = pl.ds(pl.multiple_of((2 * t + half) * count, count), count)
        y_own[:, half * piece:(half + 1) * piece] = y_all[rows]

    for copy in a_loads:
        copy.wait()
    ranks = 4 * cut
    codes = jnp.zeros((count, ranks), F32)
    for c in range(8):
        codes += lax.dot_general(
            y_all[c * count:(c + 1) * count],
            av[:, :, :, c * piece:(c + 1) * piece].reshape(ranks, piece),
            (((1,), (1,)), ((), ())),
            preferred_element_type=F32,
        )
    for h in range(2):
        code_send[h] = codes[:, h * 2 * cut:(h + 1) * 2 * cut].astype(BF16)
    fx, fhalf = f % 2, f // 2
    for step in range(4):
        for h in range(2):
            copy = remote(
                code_send.at[h], code_slot.at[fhalf, t], code_send_sem.at[step * 2 + h],
                code_recv_sem.at[fhalf * 4 + t], (f + step) % 4, 2 * fx + h,
            )
            if step == 0:
                here = t == 2 * fx + h

                @pl.when(here)
                def _():
                    code_slot[fhalf, t] = code_send[h]

                @pl.when(jnp.logical_not(here))
                def _():
                    copy.start()
            else:
                copy.start()

    def base_of(j):
        g_loads[j].wait()
        base[j, 0] = dot(y_own[...], wg[j])
        u_loads[j].wait()
        base[j, 1] = dot(y_own[...], wu[j])

    base_of(0)
    base_of(1)
    for which in range(2):
        for source in range(4):
            mine = jnp.logical_and(fx == x_at, jnp.logical_and(fhalf == which, t == source))

            @pl.when(jnp.logical_not(mine))
            def _():
                remote(
                    code_send.at[0], code_slot.at[which, source], code_send_sem.at[0],
                    code_recv_sem.at[which * 4 + source], f, x_peer,
                ).wait_recv()

    lane = lax.broadcasted_iota(jnp.int32, (count, 2 * cut), 1)
    ids = [extra[:, k:k + 1] for k in range(2)]
    for source in range(4):
        label = jnp.where(lane < cut, 2.0 * source, 2.0 * source + 1.0)
        for which in range(2):
            value = code_slot[which, source].astype(F32)
            for k in range(2):
                spread[which, k * count:(k + 1) * count, source * 2 * cut:(source + 1) * 2 * cut] = (
                    jnp.where(ids[k] == label, value, 0.0).astype(BF16)
                )

    def partial(j, which):
        right = bv[j, :, which].reshape(8 * cut, chunk)
        here = base[j, which]
        return dot(spread[which], right) + jnp.concatenate([here, here], axis=0)

    high = 2 * count
    b_loads[0].wait()
    for which in range(2):
        far_send[which * high:(which + 1) * high] = partial(0, which).astype(BF16)
    far_copy = remote(far_send, far_got, part_send_sem.at[0], part_recv_sem.at[0], f, core_peer)
    far_copy.start()
    b_loads[1].wait()
    for which in range(2):
        far_sum[which * high:(which + 1) * high] = partial(1, which)
    far_copy.wait_recv()
    x_send[...] = (far_sum[...] + far_got[...].astype(F32)).astype(BF16)
    x_copy = remote(x_send, x_got, part_send_sem.at[1], part_recv_sem.at[1], f, x_peer)
    x_copy.start()
    base_of(2)
    b_loads[2].wait()
    for which in range(2):
        near_send[which * high:(which + 1) * high] = partial(2, which).astype(BF16)
    near_copy = remote(near_send, near_got, part_send_sem.at[2], part_recv_sem.at[2], f, core_peer)
    near_copy.start()
    base_of(3)
    b_loads[3].wait()
    for which in range(2):
        near_sum[which * high:(which + 1) * high] = partial(3, which)
    near_copy.wait_recv()
    x_copy.wait_recv()
    whole = near_sum[...] + near_got[...].astype(F32) + x_got[...].astype(F32)
    first = jax.nn.sigmoid(extra[:, 2:3] - extra[:, 3:4])
    gate0, gate1 = whole[:count], whole[count:high]
    up0, up1 = whole[high:high + count], whole[high + count:]
    hidden = (
        first * (gate0 * jax.nn.sigmoid(gate0)) * up0
        + (1.0 - first) * (gate1 * jax.nn.sigmoid(gate1)) * up1
    ).astype(BF16)

    d_load.wait()
    for c in range(8):
        block = dot(hidden, wd[:, c * piece:(c + 1) * piece])
        summed[:, :, c * piece:(c + 1) * piece] = block.reshape(4, count // 4, piece)
    down_far = remote(
        summed.at[cross], down_got.at[0], down_send_sem.at[0], down_recv_sem.at[0], f, core_peer
    )
    down_near = remote(
        summed.at[core_peer], down_got.at[1], down_send_sem.at[1], down_recv_sem.at[1], f, core_peer
    )
    down_far.start()
    down_near.start()
    down_far.wait_recv()
    wide = 4 * piece
    rows = count // 4
    far_rows = summed[x_peer] + down_got[0]
    row_send[...] = jnp.concatenate([far_rows[:, :wide], far_rows[:, wide:]], axis=0).astype(BF16)
    row_copy = remote(row_send, row_got, down_send_sem.at[2], down_recv_sem.at[2], f, x_peer)
    row_copy.start()
    down_near.wait_recv()
    near_rows = summed[t] + down_got[1]
    row_copy.wait_recv()
    arrived = row_got[...].astype(F32)
    near_rows += jnp.concatenate([arrived[:rows], arrived[rows:]], axis=1)
    stacked = jnp.concatenate(
        [near_rows[:, c * piece:(c + 1) * piece] for c in range(8)], axis=0
    ).astype(BF16)
    order_out = one_hot_rows(8 * rows, lambda r: (r & 7) * 8 + (r >> 4) * 2 + ((r >> 3) & 1))
    z_send[...] = dot(order_out, stacked).astype(BF16).reshape(z_send.shape)
    z_copies = []
    for step in range(1, 4):
        to_f = (f + step) % 4
        copy = remote(
            z_send.at[to_f], z_got.at[step - 1], down_send_sem.at[2 + step],
            down_recv_sem.at[2 + step], to_f, t,
        )
        copy.start()
        z_copies.append(copy)
    total = z_send[f].astype(F32)
    for step, copy in enumerate(z_copies):
        copy.wait_recv()
        total += z_got[step].astype(F32)
    out[...] = total.astype(BF16)

    for copy in sends + [far_copy, x_copy, near_copy, down_far, down_near, row_copy] + z_copies:
        copy.wait_send()
    for step in range(4):
        for h in range(2):
            copy = remote(
                code_send.at[h], code_slot.at[fhalf, t], code_send_sem.at[step * 2 + h],
                code_recv_sem.at[fhalf * 4 + t], (f + step) % 4, 2 * fx + h,
            )
            if step == 0:

                @pl.when(jnp.logical_not(t == 2 * fx + h))
                def _():
                    copy.wait_send()
            else:
                copy.wait_send()


def fits(mesh):
    return mesh.shape["fsdp"] == 4 and mesh.shape["tok"] == 4


def fused_device(
    tokens, route_logits, expert_ids, gate_weight, up_weight, down_weight, a_factors, b_factors
):
    own, width = tokens.shape
    piece = width // 8
    depth, hidden_width = gate_weight.shape
    chunk = hidden_width // 4
    cut = b_factors.shape[2]
    count = 16 * own
    rows = count // 4
    notes = jnp.concatenate([expert_ids.astype(BF16), route_logits], axis=1)
    notes = jnp.pad(notes, ((0, 0), (0, EXTRA - notes.shape[1])))
    notes = jnp.broadcast_to(notes[:, None, :], (own, 8, EXTRA)).reshape(own * 8, EXTRA)
    pack = jnp.concatenate([tokens.reshape(own * 8, piece), notes], axis=1)
    vmem = pl.BlockSpec(memory_space=pltpu.VMEM)
    hbm = pl.BlockSpec(memory_space=pl.ANY)
    part = (4 * count, chunk)
    sems = pltpu.SemaphoreType.DMA
    out = pl.pallas_call(
        layer_kernel,
        out_shape=jax.ShapeDtypeStruct((own * 8, piece), BF16),
        in_specs=[vmem, hbm, hbm, hbm, hbm, hbm],
        out_specs=vmem,
        scratch_shapes=[
            pltpu.VMEM((4, depth, chunk), BF16),
            pltpu.VMEM((4, depth, chunk), BF16),
            pltpu.VMEM(down_weight.shape, BF16),
            pltpu.VMEM((2, 2, cut, width), BF16),
            pltpu.VMEM((4, 8, 2, cut, chunk), BF16),
            pltpu.VMEM((4, 4, own * 8, piece + EXTRA), BF16),
            pltpu.VMEM((8 * count, piece), BF16),
            pltpu.VMEM((count, depth), BF16),
            pltpu.VMEM((count, EXTRA), F32),
            pltpu.VMEM((2, count, 2 * cut), BF16),
            pltpu.VMEM((2, 4, count, 2 * cut), BF16),
            pltpu.VMEM((2, 2 * count, 8 * cut), BF16),
            pltpu.VMEM((4, 2, count, chunk), F32),
            pltpu.VMEM(part, F32),
            pltpu.VMEM(part, F32),
            pltpu.VMEM(part, BF16),
            pltpu.VMEM(part, BF16),
            pltpu.VMEM(part, BF16),
            pltpu.VMEM(part, BF16),
            pltpu.VMEM(part, BF16),
            pltpu.VMEM(part, BF16),
            pltpu.VMEM((4, rows, width), F32),
            pltpu.VMEM((2, rows, width), F32),
            pltpu.VMEM((2 * rows, width // 2), BF16),
            pltpu.VMEM((2 * rows, width // 2), BF16),
            pltpu.VMEM((4, own * 8, piece), BF16),
            pltpu.VMEM((3, own * 8, piece), BF16),
            sems((17,)),
            sems((7,)), sems((7,)), sems((8,)), sems((8,)),
            sems((3,)), sems((3,)), sems((6,)), sems((6,)),
        ],
        compiler_params=pltpu.CompilerParams(
            collective_id=0, has_side_effects=True, vmem_limit_bytes=60 * 2**20
        ),
        cost_estimate=pl.CostEstimate(
            flops=2 * count * 28 * 2**20, bytes_accessed=49 * 2**20, transcendentals=0
        ),
    )(pack, gate_weight, up_weight, down_weight, a_factors, b_factors)
    return out.reshape(own, width)


def per_device(
    tokens, route_logits, expert_ids, gate_weight, up_weight, down_weight, a_factors, b_factors
):
    tok_size = lax.axis_size("tok")
    tok_at = lax.axis_index("tok")
    experts, own_ranks, _ = a_factors.shape
    depth, width = gate_weight.shape
    cut = b_factors.shape[2]
    rank = cut * tok_size
    share = experts // tok_size

    token_here = lax.all_gather(tokens, BOTH, axis=0, tiled=True)
    logit_here = lax.all_gather(route_logits, BOTH, axis=0, tiled=True)
    ident_here = lax.all_gather(expert_ids, BOTH, axis=0, tiled=True)
    count, topk = ident_here.shape

    a_here = lax.dynamic_slice_in_dim(a_factors, tok_at * share, share, axis=0)
    partial_codes = jnp.einsum(
        "rd,ejd->erj", token_here, a_here, preferred_element_type=jnp.float32
    ).astype(jnp.bfloat16)
    whole_codes = lax.all_gather(partial_codes, "tok", axis=0, tiled=True)
    whole_codes = lax.all_gather(whole_codes, "fsdp", axis=2, tiled=True)

    token_part = lax.dynamic_slice_in_dim(token_here, tok_at * depth, depth, axis=1)
    base_gate = jnp.dot(token_part, gate_weight, preferred_element_type=jnp.float32)
    base_up = jnp.dot(token_part, up_weight, preferred_element_type=jnp.float32)
    chosen = ident_here.T[:, :, None] == jnp.arange(experts, dtype=jnp.int32)

    def delta(which):
        codes = lax.dynamic_slice_in_dim(whole_codes, which * rank + tok_at * cut, cut, axis=2)
        spread = jnp.where(chosen[:, :, :, None], codes.transpose(1, 0, 2)[None], 0)
        return jnp.dot(
            spread.reshape(topk * count, experts * cut),
            b_factors[:, which].reshape(experts * cut, width),
            preferred_element_type=jnp.float32,
        ).reshape(topk, count, width)

    both = jnp.stack([base_gate + delta(0), base_up + delta(1)])
    both = lax.psum_scatter(both, "tok", scatter_dimension=3, tiled=True)
    scores = logit_here.astype(jnp.float32)
    first = jax.nn.sigmoid(scores[:, 0] - scores[:, 1])
    mixing = jnp.stack([first, 1.0 - first], axis=0)
    hidden = jnp.sum(mixing[:, :, None] * jax.nn.silu(both[0]) * both[1], axis=0)
    summed = jnp.dot(
        hidden.astype(jnp.bfloat16), down_weight, preferred_element_type=jnp.float32
    )
    return lax.psum_scatter(summed, BOTH, scatter_dimension=0, tiled=True).astype(jnp.bfloat16)


def solution(mesh):
    placed = (
        P(("parts", "fsdp", "tok"), None),
        P(("parts", "fsdp", "tok"), None),
        P(("parts", "fsdp", "tok"), None),
        P("tok", "fsdp"),
        P("tok", "fsdp"),
        P(("fsdp", "tok"), None),
        P(None, "fsdp", None),
        P(None, None, "tok", "fsdp"),
    )
    return jax.shard_map(
        fused_device if fits(mesh) else per_device,
        mesh=mesh,
        in_specs=placed,
        out_specs=P(("parts", "fsdp", "tok"), None),
        check_vma=False,
    )
```

```python
import jax
import jax.numpy as jnp
from jax import lax
from jax.experimental import pallas as pl
from jax.experimental.pallas import tpu as pltpu
from jax.sharding import PartitionSpec as P

BOTH = ("fsdp", "tok")
MESH = pl.DeviceIdType.MESH
F32, BF16 = jnp.float32, jnp.bfloat16
EXTRA = 128


def one_hot_rows(rows, source_of):
    row = lax.broadcasted_iota(jnp.int32, (rows, rows), 0)
    column = lax.broadcasted_iota(jnp.int32, (rows, rows), 1)
    return jnp.where(column == source_of(row), 1.0, 0.0).astype(BF16)


def dot(left, right):
    return jnp.dot(left, right, preferred_element_type=F32)


def layer_kernel(
    tokens, logits, ids_in, wg_hbm, wu_hbm, wd_hbm, a_hbm, b_hbm, out,
    pack, wg, wu, wd, av, bv, held, y_all, y_own, extra, code_send, code_slot, spread,
    base, far_sum, near_sum, near_send, far_send, x_send, near_got, far_got, x_got,
    summed, down_got, row_send, row_got, z_send, z_got,
    load_sem, tok_send_sem, tok_recv_sem, code_send_sem, code_recv_sem,
    part_send_sem, part_recv_sem, down_send_sem, down_recv_sem,
):
    f, t = lax.axis_index("fsdp"), lax.axis_index("tok")
    core_peer, x_peer, cross = (5 - t) % 4, (t + 2) % 4, 3 - t
    x_at = t // 2
    piece = pack.shape[1] - EXTRA
    depth, chunk = wg.shape[1], wg.shape[2]
    cut = b_hbm.shape[2]
    count = y_own.shape[0]
    order = (cross, x_peer, core_peer, t)

    def columns(j):
        return pl.ds(pl.multiple_of(order[j] * chunk, chunk), chunk)

    def load(index, source, target):
        return pltpu.make_async_copy(source, target, load_sem.at[index])

    def remote(source, target, send, recv, to_f, to_t):
        return pltpu.make_async_remote_copy(
            src_ref=source, dst_ref=target, send_sem=send, recv_sem=recv,
            device_id={"fsdp": to_f, "tok": to_t}, device_id_type=MESH,
        )

    a_loads = [
        load(2 * h + e, a_hbm.at[2 * t + e, pl.ds(h * cut, cut)], av.at[h, e])
        for h in range(2) for e in range(2)
    ]
    g_loads = [load(4 + j, wg_hbm.at[:, columns(j)], wg.at[j]) for j in range(4)]
    u_loads = [load(8 + j, wu_hbm.at[:, columns(j)], wu.at[j]) for j in range(4)]
    b_loads = [load(12 + j, b_hbm.at[:, :, :, columns(j)], bv.at[j]) for j in range(4)]
    d_load = load(16, wd_hbm, wd)
    for copy in a_loads + [g_loads[0], u_loads[0], g_loads[1], u_loads[1], b_loads[0], b_loads[1]]:
        copy.start()

    barrier = pltpu.get_barrier_semaphore()
    for to_f, to_t in [((f + 1) % 4, t), ((f + 2) % 4, t), ((f + 3) % 4, t), (f, core_peer), (f, x_peer)]:
        pl.semaphore_signal(
            barrier, inc=1, device_id={"fsdp": to_f, "tok": to_t}, device_id_type=MESH
        )
    mine = tokens[...].astype(F32)
    own = mine.shape[0]
    pack[:, :piece] = jnp.concatenate(
        [mine[:, c * piece:(c + 1) * piece] for c in range(8)], axis=0
    ).astype(BF16)
    lanes = lax.broadcasted_iota(jnp.int32, (own, EXTRA), 1)
    notes = jnp.zeros((own, EXTRA), F32)
    for k in range(2):
        notes = jnp.where(lanes == k, ids_in[...].astype(F32)[:, k:k + 1], notes)
        notes = jnp.where(lanes == 2 + k, logits[...].astype(F32)[:, k:k + 1], notes)
    pack[:, piece:] = jnp.concatenate([notes, jnp.zeros((7 * own, EXTRA), F32)], axis=0).astype(BF16)
    held[t, f] = pack[...]
    pl.semaphore_wait(barrier, 5)

    sends = []
    for step in range(1, 4):
        copy = remote(
            pack, held.at[t, f], tok_send_sem.at[step], tok_recv_sem.at[step], (f + step) % 4, t
        )
        copy.start()
        sends.append(copy)
    for copy in sends:
        copy.wait_recv()
    to_core = remote(held.at[t], held.at[t], tok_send_sem.at[4], tok_recv_sem.at[4], f, core_peer)
    to_x = remote(held.at[t], held.at[t], tok_send_sem.at[5], tok_recv_sem.at[5], f, x_peer)
    to_x.start()
    to_core.start()
    to_x.wait_recv()
    onward = remote(
        held.at[x_peer], held.at[x_peer], tok_send_sem.at[6], tok_recv_sem.at[6], f, core_peer
    )
    onward.start()
    sends += [to_core, to_x, onward]
    to_core.wait_recv()
    onward.wait_recv()
    for copy in [g_loads[2], u_loads[2], b_loads[2], g_loads[3], u_loads[3], b_loads[3], d_load]:
        copy.start()

    order_in = one_hot_rows(
        8 * count, lambda r: ((r & 31) >> 1) * 16 + (r >> 5) * 2 + (r & 1)
    )
    turned = dot(order_in, held[...].reshape(8 * count, piece + EXTRA))
    y_all[...] = turned[:, :piece].astype(BF16)
    extra[...] = turned[:count, piece:]
    for half in range(2):
        rows = pl.ds(pl.multiple_of((2 * t + half) * count, count), count)
        y_own[:, half * piece:(half + 1) * piece] = y_all[rows]

    for copy in a_loads:
        copy.wait()
    ranks = 4 * cut
    codes = jnp.zeros((count, ranks), F32)
    for c in range(8):
        codes += lax.dot_general(
            y_all[c * count:(c + 1) * count],
            av[:, :, :, c * piece:(c + 1) * piece].reshape(ranks, piece),
            (((1,), (1,)), ((), ())),
            preferred_element_type=F32,
        )
    for h in range(2):
        code_send[h] = codes[:, h * 2 * cut:(h + 1) * 2 * cut].astype(BF16)
    fx, fhalf = f % 2, f // 2
    for step in range(4):
        for h in range(2):
            copy = remote(
                code_send.at[h], code_slot.at[fhalf, t], code_send_sem.at[step * 2 + h],
                code_recv_sem.at[fhalf * 4 + t], (f + step) % 4, 2 * fx + h,
            )
            if step == 0:
                here = t == 2 * fx + h

                @pl.when(here)
                def _():
                    code_slot[fhalf, t] = code_send[h]

                @pl.when(jnp.logical_not(here))
                def _():
                    copy.start()
            else:
                copy.start()

    def base_of(j):
        g_loads[j].wait()
        base[j, 0] = dot(y_own[...], wg[j])
        u_loads[j].wait()
        base[j, 1] = dot(y_own[...], wu[j])

    base_of(0)
    base_of(1)
    for which in range(2):
        for source in range(4):
            mine = jnp.logical_and(fx == x_at, jnp.logical_and(fhalf == which, t == source))

            @pl.when(jnp.logical_not(mine))
            def _():
                remote(
                    code_send.at[0], code_slot.at[which, source], code_send_sem.at[0],
                    code_recv_sem.at[which * 4 + source], f, x_peer,
                ).wait_recv()

    lane = lax.broadcasted_iota(jnp.int32, (count, 2 * cut), 1)
    ids = [extra[:, k:k + 1] for k in range(2)]
    for source in range(4):
        label = jnp.where(lane < cut, 2.0 * source, 2.0 * source + 1.0)
        for which in range(2):
            value = code_slot[which, source].astype(F32)
            for k in range(2):
                spread[which, k * count:(k + 1) * count, source * 2 * cut:(source + 1) * 2 * cut] = (
                    jnp.where(ids[k] == label, value, 0.0).astype(BF16)
                )

    def partial(j, which):
        right = bv[j, :, which].reshape(8 * cut, chunk)
        here = base[j, which]
        return dot(spread[which], right) + jnp.concatenate([here, here], axis=0)

    high = 2 * count
    b_loads[0].wait()
    for which in range(2):
        far_send[which * high:(which + 1) * high] = partial(0, which).astype(BF16)
    far_copy = remote(far_send, far_got, part_send_sem.at[0], part_recv_sem.at[0], f, core_peer)
    far_copy.start()
    b_loads[1].wait()
    for which in range(2):
        far_sum[which * high:(which + 1) * high] = partial(1, which)
    far_copy.wait_recv()
    x_send[...] = (far_sum[...] + far_got[...].astype(F32)).astype(BF16)
    x_copy = remote(x_send, x_got, part_send_sem.at[1], part_recv_sem.at[1], f, x_peer)
    x_copy.start()
    base_of(2)
    b_loads[2].wait()
    for which in range(2):
        near_send[which * high:(which + 1) * high] = partial(2, which).astype(BF16)
    near_copy = remote(near_send, near_got, part_send_sem.at[2], part_recv_sem.at[2], f, core_peer)
    near_copy.start()
    base_of(3)
    b_loads[3].wait()
    for which in range(2):
        near_sum[which * high:(which + 1) * high] = partial(3, which)
    near_copy.wait_recv()
    x_copy.wait_recv()
    whole = near_sum[...] + near_got[...].astype(F32) + x_got[...].astype(F32)
    first = jax.nn.sigmoid(extra[:, 2:3] - extra[:, 3:4])
    gate0, gate1 = whole[:count], whole[count:high]
    up0, up1 = whole[high:high + count], whole[high + count:]
    hidden = (
        first * (gate0 * jax.nn.sigmoid(gate0)) * up0
        + (1.0 - first) * (gate1 * jax.nn.sigmoid(gate1)) * up1
    ).astype(BF16)

    d_load.wait()
    rows, wide, small = count // 4, 4 * piece, piece // 2
    to_core_copies = []
    for half in range(2):
        for c in range(4):
            at = half * wide + c * piece
            block = dot(hidden, wd[:, at:at + piece])
            summed[half, :, :, c * piece:(c + 1) * piece] = block.reshape(4, rows, piece)
        pair = []
        for which, source in enumerate((cross, core_peer)):
            index = 2 * half + which
            copy = remote(
                summed.at[half, source], down_got.at[half, which],
                down_send_sem.at[index], down_recv_sem.at[index], f, core_peer,
            )
            copy.start()
            pair.append(copy)
        to_core_copies.append(pair)
    row_copies = []
    for half in range(2):
        to_core_copies[half][0].wait_recv()
        far_rows = summed[half, x_peer] + down_got[half, 0]
        row_send[half] = jnp.concatenate(
            [far_rows[:, :wide // 2], far_rows[:, wide // 2:]], axis=0
        ).astype(BF16)
        copy = remote(
            row_send.at[half], row_got.at[half],
            down_send_sem.at[4 + half], down_recv_sem.at[4 + half], f, x_peer,
        )
        copy.start()
        row_copies.append(copy)
    order_out = one_hot_rows(8 * rows, lambda r: ((r >> 1) & 7) * 8 + (r >> 4) * 2 + (r & 1))
    z_copies = []
    for half in range(2):
        to_core_copies[half][1].wait_recv()
        near_rows = summed[half, t] + down_got[half, 1]
        row_copies[half].wait_recv()
        arrived = row_got[half].astype(F32)
        near_rows += jnp.concatenate([arrived[:rows], arrived[rows:]], axis=1)
        stacked = jnp.concatenate(
            [near_rows[:, c * small:(c + 1) * small] for c in range(8)], axis=0
        ).astype(BF16)
        z_send[half] = dot(order_out, stacked).astype(BF16).reshape(4, 2 * rows, small)
        for step in range(1, 4):
            to_f = (f + step) % 4
            index = 5 + 3 * half + step
            copy = remote(
                z_send.at[half, to_f], z_got.at[half, step - 1],
                down_send_sem.at[index], down_recv_sem.at[index], to_f, t,
            )
            copy.start()
            z_copies.append(copy)
    for half in range(2):
        total = z_send[half, f].astype(F32)
        for step in range(3):
            z_copies[3 * half + step].wait_recv()
            total += z_got[half, step].astype(F32)
        out[:, half * wide:(half + 1) * wide] = jnp.concatenate(
            [total[own * c:own * (c + 1)] for c in range(8)], axis=1
        ).astype(BF16)

    for copy in sends + [far_copy, x_copy, near_copy] + row_copies + z_copies:
        copy.wait_send()
    for pair in to_core_copies:
        for copy in pair:
            copy.wait_send()
    for step in range(4):
        for h in range(2):
            copy = remote(
                code_send.at[h], code_slot.at[fhalf, t], code_send_sem.at[step * 2 + h],
                code_recv_sem.at[fhalf * 4 + t], (f + step) % 4, 2 * fx + h,
            )
            if step == 0:

                @pl.when(jnp.logical_not(t == 2 * fx + h))
                def _():
                    copy.wait_send()
            else:
                copy.wait_send()


def fits(mesh):
    return mesh.shape["fsdp"] == 4 and mesh.shape["tok"] == 4


def fused_device(
    tokens, route_logits, expert_ids, gate_weight, up_weight, down_weight, a_factors, b_factors
):
    own, width = tokens.shape
    piece = width // 8
    depth, hidden_width = gate_weight.shape
    chunk = hidden_width // 4
    cut = b_factors.shape[2]
    count = 16 * own
    rows = count // 4
    vmem = pl.BlockSpec(memory_space=pltpu.VMEM)
    hbm = pl.BlockSpec(memory_space=pl.ANY)
    part = (4 * count, chunk)
    sems = pltpu.SemaphoreType.DMA
    out = pl.pallas_call(
        layer_kernel,
        out_shape=jax.ShapeDtypeStruct((own, width), BF16),
        in_specs=[vmem, vmem, vmem, hbm, hbm, hbm, hbm, hbm],
        out_specs=vmem,
        scratch_shapes=[
            pltpu.VMEM((own * 8, piece + EXTRA), BF16),
            pltpu.VMEM((4, depth, chunk), BF16),
            pltpu.VMEM((4, depth, chunk), BF16),
            pltpu.VMEM(down_weight.shape, BF16),
            pltpu.VMEM((2, 2, cut, width), BF16),
            pltpu.VMEM((4, 8, 2, cut, chunk), BF16),
            pltpu.VMEM((4, 4, own * 8, piece + EXTRA), BF16),
            pltpu.VMEM((8 * count, piece), BF16),
            pltpu.VMEM((count, depth), BF16),
            pltpu.VMEM((count, EXTRA), F32),
            pltpu.VMEM((2, count, 2 * cut), BF16),
            pltpu.VMEM((2, 4, count, 2 * cut), BF16),
            pltpu.VMEM((2, 2 * count, 8 * cut), BF16),
            pltpu.VMEM((4, 2, count, chunk), F32),
            pltpu.VMEM(part, F32),
            pltpu.VMEM(part, F32),
            pltpu.VMEM(part, BF16),
            pltpu.VMEM(part, BF16),
            pltpu.VMEM(part, BF16),
            pltpu.VMEM(part, BF16),
            pltpu.VMEM(part, BF16),
            pltpu.VMEM(part, BF16),
            pltpu.VMEM((2, 4, rows, width // 2), F32),
            pltpu.VMEM((2, 2, rows, width // 2), F32),
            pltpu.VMEM((2, 2 * rows, width // 4), BF16),
            pltpu.VMEM((2, 2 * rows, width // 4), BF16),
            pltpu.VMEM((2, 4, own * 8, piece // 2), BF16),
            pltpu.VMEM((2, 3, own * 8, piece // 2), BF16),
            sems((17,)),
            sems((7,)), sems((7,)), sems((8,)), sems((8,)),
            sems((3,)), sems((3,)), sems((12,)), sems((12,)),
        ],
        compiler_params=pltpu.CompilerParams(
            collective_id=0, has_side_effects=True, vmem_limit_bytes=60 * 2**20
        ),
        cost_estimate=pl.CostEstimate(
            flops=2 * count * 28 * 2**20, bytes_accessed=49 * 2**20, transcendentals=0
        ),
    )(
        tokens, route_logits, expert_ids,
        gate_weight, up_weight, down_weight, a_factors, b_factors,
    )
    return out


def per_device(
    tokens, route_logits, expert_ids, gate_weight, up_weight, down_weight, a_factors, b_factors
):
    tok_size = lax.axis_size("tok")
    tok_at = lax.axis_index("tok")
    experts, own_ranks, _ = a_factors.shape
    depth, width = gate_weight.shape
    cut = b_factors.shape[2]
    rank = cut * tok_size
    share = experts // tok_size

    token_here = lax.all_gather(tokens, BOTH, axis=0, tiled=True)
    logit_here = lax.all_gather(route_logits, BOTH, axis=0, tiled=True)
    ident_here = lax.all_gather(expert_ids, BOTH, axis=0, tiled=True)
    count, topk = ident_here.shape

    a_here = lax.dynamic_slice_in_dim(a_factors, tok_at * share, share, axis=0)
    partial_codes = jnp.einsum(
        "rd,ejd->erj", token_here, a_here, preferred_element_type=jnp.float32
    ).astype(jnp.bfloat16)
    whole_codes = lax.all_gather(partial_codes, "tok", axis=0, tiled=True)
    whole_codes = lax.all_gather(whole_codes, "fsdp", axis=2, tiled=True)

    token_part = lax.dynamic_slice_in_dim(token_here, tok_at * depth, depth, axis=1)
    base_gate = jnp.dot(token_part, gate_weight, preferred_element_type=jnp.float32)
    base_up = jnp.dot(token_part, up_weight, preferred_element_type=jnp.float32)
    chosen = ident_here.T[:, :, None] == jnp.arange(experts, dtype=jnp.int32)

    def delta(which):
        codes = lax.dynamic_slice_in_dim(whole_codes, which * rank + tok_at * cut, cut, axis=2)
        spread = jnp.where(chosen[:, :, :, None], codes.transpose(1, 0, 2)[None], 0)
        return jnp.dot(
            spread.reshape(topk * count, experts * cut),
            b_factors[:, which].reshape(experts * cut, width),
            preferred_element_type=jnp.float32,
        ).reshape(topk, count, width)

    both = jnp.stack([base_gate + delta(0), base_up + delta(1)])
    both = lax.psum_scatter(both, "tok", scatter_dimension=3, tiled=True)
    scores = logit_here.astype(jnp.float32)
    first = jax.nn.sigmoid(scores[:, 0] - scores[:, 1])
    mixing = jnp.stack([first, 1.0 - first], axis=0)
    hidden = jnp.sum(mixing[:, :, None] * jax.nn.silu(both[0]) * both[1], axis=0)
    summed = jnp.dot(
        hidden.astype(jnp.bfloat16), down_weight, preferred_element_type=jnp.float32
    )
    return lax.psum_scatter(summed, BOTH, scatter_dimension=0, tiled=True).astype(jnp.bfloat16)


def solution(mesh):
    placed = (
        P(("parts", "fsdp", "tok"), None),
        P(("parts", "fsdp", "tok"), None),
        P(("parts", "fsdp", "tok"), None),
        P("tok", "fsdp"),
        P("tok", "fsdp"),
        P(("fsdp", "tok"), None),
        P(None, "fsdp", None),
        P(None, None, "tok", "fsdp"),
    )
    return jax.shard_map(
        fused_device if fits(mesh) else per_device,
        mesh=mesh,
        in_specs=placed,
        out_specs=P(("parts", "fsdp", "tok"), None),
        check_vma=False,
    )
```

```python
import jax
import jax.numpy as jnp
from jax import lax
from jax.experimental import pallas as pl
from jax.experimental.pallas import tpu as pltpu
from jax.sharding import PartitionSpec as P

BOTH = ("fsdp", "tok")
MESH = pl.DeviceIdType.MESH
F32, BF16 = jnp.float32, jnp.bfloat16
EXTRA = 128


def one_hot_rows(rows, source_of):
    row = lax.broadcasted_iota(jnp.int32, (rows, rows), 0)
    column = lax.broadcasted_iota(jnp.int32, (rows, rows), 1)
    return jnp.where(column == source_of(row), 1.0, 0.0).astype(BF16)


def dot(left, right):
    return jnp.dot(left, right, preferred_element_type=F32)


def layer_kernel(
    tokens, logits, ids_in, wg_hbm, wu_hbm, wd_hbm, a_hbm, b_hbm, out,
    pack, wg, wu, wd, av, bv, held, y_all, y_own, extra, code_send, code_slot, spread,
    base, near_sum, near_send, far_send, x_send, near_got, far_got, x_got,
    summed, down_got, row_send, row_got, z_send, z_got,
    load_sem, tok_send_sem, tok_recv_sem, code_send_sem, code_recv_sem,
    part_send_sem, part_recv_sem, down_send_sem, down_recv_sem,
):
    f, t = lax.axis_index("fsdp"), lax.axis_index("tok")
    core_peer, x_peer, cross = (5 - t) % 4, (t + 2) % 4, 3 - t
    x_at = t // 2
    piece = pack.shape[1] - EXTRA
    depth, chunk = wg.shape[1], wg.shape[2]
    cut = b_hbm.shape[2]
    count = y_own.shape[0]
    order = (cross, x_peer, core_peer, t)

    def columns(j):
        return pl.ds(pl.multiple_of(order[j] * chunk, chunk), chunk)

    def load(index, source, target):
        return pltpu.make_async_copy(source, target, load_sem.at[index])

    def remote(source, target, send, recv, to_f, to_t):
        return pltpu.make_async_remote_copy(
            src_ref=source, dst_ref=target, send_sem=send, recv_sem=recv,
            device_id={"fsdp": to_f, "tok": to_t}, device_id_type=MESH,
        )

    a_loads = [
        load(2 * h + e, a_hbm.at[2 * t + e, pl.ds(h * cut, cut)], av.at[h, e])
        for h in range(2) for e in range(2)
    ]
    g_loads = [load(4 + j, wg_hbm.at[:, columns(j)], wg.at[j]) for j in range(4)]
    u_loads = [load(8 + j, wu_hbm.at[:, columns(j)], wu.at[j]) for j in range(4)]
    b_loads = [load(12 + j, b_hbm.at[:, :, :, columns(j)], bv.at[j]) for j in range(4)]
    d_load = load(16, wd_hbm, wd)
    for copy in a_loads + [g_loads[0], u_loads[0], g_loads[1], u_loads[1], b_loads[0], b_loads[1]]:
        copy.start()

    barrier = pltpu.get_barrier_semaphore()
    for to_f, to_t in [((f + 1) % 4, t), ((f + 2) % 4, t), ((f + 3) % 4, t), (f, core_peer), (f, x_peer)]:
        pl.semaphore_signal(
            barrier, inc=1, device_id={"fsdp": to_f, "tok": to_t}, device_id_type=MESH
        )
    mine = tokens[...].astype(F32)
    own = mine.shape[0]
    pack[:, :piece] = jnp.concatenate(
        [mine[:, c * piece:(c + 1) * piece] for c in range(8)], axis=0
    ).astype(BF16)
    lanes = lax.broadcasted_iota(jnp.int32, (own, EXTRA), 1)
    notes = jnp.zeros((own, EXTRA), F32)
    for k in range(2):
        notes = jnp.where(lanes == k, ids_in[...].astype(F32)[:, k:k + 1], notes)
        notes = jnp.where(lanes == 2 + k, logits[...].astype(F32)[:, k:k + 1], notes)
    pack[:, piece:] = jnp.concatenate([notes, jnp.zeros((7 * own, EXTRA), F32)], axis=0).astype(BF16)
    held[t, f] = pack[...]
    pl.semaphore_wait(barrier, 5)

    sends = []
    for step in range(1, 4):
        copy = remote(
            pack, held.at[t, f], tok_send_sem.at[step], tok_recv_sem.at[step], (f + step) % 4, t
        )
        copy.start()
        sends.append(copy)
    along_x, along_core, onward = [], [], []
    for step in (0, 1, 3, 2):
        if step:
            sends[step - 1].wait_recv()
        block = held.at[t, (f + 4 - step) % 4]
        to_x = remote(
            block, block, tok_send_sem.at[4 + step], tok_recv_sem.at[4 + step], f, x_peer
        )
        to_core = remote(
            block, block, tok_send_sem.at[8 + step], tok_recv_sem.at[8 + step], f, core_peer
        )
        to_x.start()
        to_core.start()
        along_x.append(to_x)
        along_core.append(to_core)
    for place, step in enumerate((0, 1, 3, 2)):
        along_x[place].wait_recv()
        block = held.at[x_peer, (f + 4 - step) % 4]
        copy = remote(
            block, block, tok_send_sem.at[12 + step], tok_recv_sem.at[12 + step], f, core_peer
        )
        copy.start()
        onward.append(copy)
    for copy in along_core + onward:
        copy.wait_recv()
    sends += along_x + along_core + onward
    for copy in [g_loads[2], u_loads[2], b_loads[2], g_loads[3], u_loads[3], b_loads[3], d_load]:
        copy.start()

    order_in = one_hot_rows(
        8 * count, lambda r: ((r & 31) >> 1) * 16 + (r >> 5) * 2 + (r & 1)
    )
    turned = dot(order_in, held[...].reshape(8 * count, piece + EXTRA))
    y_all[...] = turned[:, :piece].astype(BF16)
    extra[...] = turned[:count, piece:]
    for half in range(2):
        rows = pl.ds(pl.multiple_of((2 * t + half) * count, count), count)
        y_own[:, half * piece:(half + 1) * piece] = y_all[rows]

    for copy in a_loads:
        copy.wait()
    ranks = 4 * cut
    codes = jnp.zeros((count, ranks), F32)
    for c in range(8):
        codes += lax.dot_general(
            y_all[c * count:(c + 1) * count],
            av[:, :, :, c * piece:(c + 1) * piece].reshape(ranks, piece),
            (((1,), (1,)), ((), ())),
            preferred_element_type=F32,
        )
    for h in range(2):
        code_send[h] = codes[:, h * 2 * cut:(h + 1) * 2 * cut].astype(BF16)
    fx, fhalf = f % 2, f // 2
    for step in range(4):
        for h in range(2):
            copy = remote(
                code_send.at[h], code_slot.at[fhalf, t], code_send_sem.at[step * 2 + h],
                code_recv_sem.at[fhalf * 4 + t], (f + step) % 4, 2 * fx + h,
            )
            if step == 0:
                here = t == 2 * fx + h

                @pl.when(here)
                def _():
                    code_slot[fhalf, t] = code_send[h]

                @pl.when(jnp.logical_not(here))
                def _():
                    copy.start()
            else:
                copy.start()

    def base_of(j):
        g_loads[j].wait()
        base[j, 0] = dot(y_own[...], wg[j])
        u_loads[j].wait()
        base[j, 1] = dot(y_own[...], wu[j])

    base_of(0)
    base_of(1)
    for which in range(2):
        for source in range(4):
            mine = jnp.logical_and(fx == x_at, jnp.logical_and(fhalf == which, t == source))

            @pl.when(jnp.logical_not(mine))
            def _():
                remote(
                    code_send.at[0], code_slot.at[which, source], code_send_sem.at[0],
                    code_recv_sem.at[which * 4 + source], f, x_peer,
                ).wait_recv()

    lane = lax.broadcasted_iota(jnp.int32, (count, 2 * cut), 1)
    ids = [extra[:, k:k + 1] for k in range(2)]
    for source in range(4):
        label = jnp.where(lane < cut, 2.0 * source, 2.0 * source + 1.0)
        for which in range(2):
            value = code_slot[which, source].astype(F32)
            for k in range(2):
                spread[which, k * count:(k + 1) * count, source * 2 * cut:(source + 1) * 2 * cut] = (
                    jnp.where(ids[k] == label, value, 0.0).astype(BF16)
                )

    def partial(j, which):
        right = bv[j, :, which].reshape(8 * cut, chunk)
        here = base[j, which]
        return dot(spread[which], right) + jnp.concatenate([here, here], axis=0)

    high = 2 * count
    part_copies = []

    def part_copy(source, target, kind, which, to_t):
        at = pl.ds(which * high, high)
        index = 2 * kind + which
        copy = remote(
            source.at[at], target.at[at], part_send_sem.at[index], part_recv_sem.at[index], f, to_t
        )
        copy.start()
        part_copies.append(copy)
        return copy

    b_loads[0].wait()
    b_loads[1].wait()
    far_copies, x_copies, near_copies = [], [], []
    for which in range(2):
        at = slice(which * high, (which + 1) * high)
        far_send[at] = partial(0, which).astype(BF16)
        far_copies.append(part_copy(far_send, far_got, 0, which, core_peer))
    for which in range(2):
        at = slice(which * high, (which + 1) * high)
        own_sum = partial(1, which)
        far_copies[which].wait_recv()
        x_send[at] = (own_sum + far_got[at].astype(F32)).astype(BF16)
        x_copies.append(part_copy(x_send, x_got, 1, which, x_peer))
    base_of(2)
    b_loads[2].wait()
    for which in range(2):
        near_send[which * high:(which + 1) * high] = partial(2, which).astype(BF16)
        near_copies.append(part_copy(near_send, near_got, 2, which, core_peer))
    base_of(3)
    b_loads[3].wait()
    for which in range(2):
        near_sum[which * high:(which + 1) * high] = partial(3, which)
    for copy in near_copies + x_copies:
        copy.wait_recv()
    whole = near_sum[...] + near_got[...].astype(F32) + x_got[...].astype(F32)
    first = jax.nn.sigmoid(extra[:, 2:3] - extra[:, 3:4])
    gate0, gate1 = whole[:count], whole[count:high]
    up0, up1 = whole[high:high + count], whole[high + count:]
    hidden = (
        first * (gate0 * jax.nn.sigmoid(gate0)) * up0
        + (1.0 - first) * (gate1 * jax.nn.sigmoid(gate1)) * up1
    ).astype(BF16)

    d_load.wait()
    rows, wide, small = count // 4, 4 * piece, piece // 2
    to_core_copies = []
    for half in range(2):
        for c in range(4):
            at = half * wide + c * piece
            block = dot(hidden, wd[:, at:at + piece])
            summed[half, :, :, c * piece:(c + 1) * piece] = block.reshape(4, rows, piece)
        pair = []
        for which, source in enumerate((cross, core_peer)):
            index = 2 * half + which
            copy = remote(
                summed.at[half, source], down_got.at[half, which],
                down_send_sem.at[index], down_recv_sem.at[index], f, core_peer,
            )
            copy.start()
            pair.append(copy)
        to_core_copies.append(pair)
    row_copies = []
    for half in range(2):
        to_core_copies[half][0].wait_recv()
        far_rows = summed[half, x_peer] + down_got[half, 0]
        row_send[half] = jnp.concatenate(
            [far_rows[:, :wide // 2], far_rows[:, wide // 2:]], axis=0
        ).astype(BF16)
        copy = remote(
            row_send.at[half], row_got.at[half],
            down_send_sem.at[4 + half], down_recv_sem.at[4 + half], f, x_peer,
        )
        copy.start()
        row_copies.append(copy)
    order_out = one_hot_rows(8 * rows, lambda r: ((r >> 1) & 7) * 8 + (r >> 4) * 2 + (r & 1))
    z_copies = []
    for half in range(2):
        to_core_copies[half][1].wait_recv()
        near_rows = summed[half, t] + down_got[half, 1]
        row_copies[half].wait_recv()
        arrived = row_got[half].astype(F32)
        near_rows += jnp.concatenate([arrived[:rows], arrived[rows:]], axis=1)
        stacked = jnp.concatenate(
            [near_rows[:, c * small:(c + 1) * small] for c in range(8)], axis=0
        ).astype(BF16)
        z_send[half] = dot(order_out, stacked).astype(BF16).reshape(4, 2 * rows, small)
        for step in range(1, 4):
            to_f = (f + step) % 4
            index = 5 + 3 * half + step
            copy = remote(
                z_send.at[half, to_f], z_got.at[half, step - 1],
                down_send_sem.at[index], down_recv_sem.at[index], to_f, t,
            )
            copy.start()
            z_copies.append(copy)
    for half in range(2):
        total = z_send[half, f].astype(F32)
        for step in range(3):
            z_copies[3 * half + step].wait_recv()
            total += z_got[half, step].astype(F32)
        out[:, half * wide:(half + 1) * wide] = jnp.concatenate(
            [total[own * c:own * (c + 1)] for c in range(8)], axis=1
        ).astype(BF16)

    for copy in sends + part_copies + row_copies + z_copies:
        copy.wait_send()
    for pair in to_core_copies:
        for copy in pair:
            copy.wait_send()
    for step in range(4):
        for h in range(2):
            copy = remote(
                code_send.at[h], code_slot.at[fhalf, t], code_send_sem.at[step * 2 + h],
                code_recv_sem.at[fhalf * 4 + t], (f + step) % 4, 2 * fx + h,
            )
            if step == 0:

                @pl.when(jnp.logical_not(t == 2 * fx + h))
                def _():
                    copy.wait_send()
            else:
                copy.wait_send()


def fits(mesh):
    return mesh.shape["fsdp"] == 4 and mesh.shape["tok"] == 4


def fused_device(
    tokens, route_logits, expert_ids, gate_weight, up_weight, down_weight, a_factors, b_factors
):
    own, width = tokens.shape
    piece = width // 8
    depth, hidden_width = gate_weight.shape
    chunk = hidden_width // 4
    cut = b_factors.shape[2]
    count = 16 * own
    rows = count // 4
    vmem = pl.BlockSpec(memory_space=pltpu.VMEM)
    hbm = pl.BlockSpec(memory_space=pl.ANY)
    part = (4 * count, chunk)
    sems = pltpu.SemaphoreType.DMA
    out = pl.pallas_call(
        layer_kernel,
        out_shape=jax.ShapeDtypeStruct((own, width), BF16),
        in_specs=[vmem, vmem, vmem, hbm, hbm, hbm, hbm, hbm],
        out_specs=vmem,
        scratch_shapes=[
            pltpu.VMEM((own * 8, piece + EXTRA), BF16),
            pltpu.VMEM((4, depth, chunk), BF16),
            pltpu.VMEM((4, depth, chunk), BF16),
            pltpu.VMEM(down_weight.shape, BF16),
            pltpu.VMEM((2, 2, cut, width), BF16),
            pltpu.VMEM((4, 8, 2, cut, chunk), BF16),
            pltpu.VMEM((4, 4, own * 8, piece + EXTRA), BF16),
            pltpu.VMEM((8 * count, piece), BF16),
            pltpu.VMEM((count, depth), BF16),
            pltpu.VMEM((count, EXTRA), F32),
            pltpu.VMEM((2, count, 2 * cut), BF16),
            pltpu.VMEM((2, 4, count, 2 * cut), BF16),
            pltpu.VMEM((2, 2 * count, 8 * cut), BF16),
            pltpu.VMEM((4, 2, count, chunk), F32),
            pltpu.VMEM(part, F32),
            pltpu.VMEM(part, BF16),
            pltpu.VMEM(part, BF16),
            pltpu.VMEM(part, BF16),
            pltpu.VMEM(part, BF16),
            pltpu.VMEM(part, BF16),
            pltpu.VMEM(part, BF16),
            pltpu.VMEM((2, 4, rows, width // 2), F32),
            pltpu.VMEM((2, 2, rows, width // 2), F32),
            pltpu.VMEM((2, 2 * rows, width // 4), BF16),
            pltpu.VMEM((2, 2 * rows, width // 4), BF16),
            pltpu.VMEM((2, 4, own * 8, piece // 2), BF16),
            pltpu.VMEM((2, 3, own * 8, piece // 2), BF16),
            sems((17,)),
            sems((16,)), sems((16,)), sems((8,)), sems((8,)),
            sems((6,)), sems((6,)), sems((12,)), sems((12,)),
        ],
        compiler_params=pltpu.CompilerParams(
            collective_id=0, has_side_effects=True, vmem_limit_bytes=60 * 2**20
        ),
        cost_estimate=pl.CostEstimate(
            flops=2 * count * 28 * 2**20, bytes_accessed=49 * 2**20, transcendentals=0
        ),
    )(
        tokens, route_logits, expert_ids,
        gate_weight, up_weight, down_weight, a_factors, b_factors,
    )
    return out


def per_device(
    tokens, route_logits, expert_ids, gate_weight, up_weight, down_weight, a_factors, b_factors
):
    tok_size = lax.axis_size("tok")
    tok_at = lax.axis_index("tok")
    experts, own_ranks, _ = a_factors.shape
    depth, width = gate_weight.shape
    cut = b_factors.shape[2]
    rank = cut * tok_size
    share = experts // tok_size

    token_here = lax.all_gather(tokens, BOTH, axis=0, tiled=True)
    logit_here = lax.all_gather(route_logits, BOTH, axis=0, tiled=True)
    ident_here = lax.all_gather(expert_ids, BOTH, axis=0, tiled=True)
    count, topk = ident_here.shape

    a_here = lax.dynamic_slice_in_dim(a_factors, tok_at * share, share, axis=0)
    partial_codes = jnp.einsum(
        "rd,ejd->erj", token_here, a_here, preferred_element_type=jnp.float32
    ).astype(jnp.bfloat16)
    whole_codes = lax.all_gather(partial_codes, "tok", axis=0, tiled=True)
    whole_codes = lax.all_gather(whole_codes, "fsdp", axis=2, tiled=True)

    token_part = lax.dynamic_slice_in_dim(token_here, tok_at * depth, depth, axis=1)
    base_gate = jnp.dot(token_part, gate_weight, preferred_element_type=jnp.float32)
    base_up = jnp.dot(token_part, up_weight, preferred_element_type=jnp.float32)
    chosen = ident_here.T[:, :, None] == jnp.arange(experts, dtype=jnp.int32)

    def delta(which):
        codes = lax.dynamic_slice_in_dim(whole_codes, which * rank + tok_at * cut, cut, axis=2)
        spread = jnp.where(chosen[:, :, :, None], codes.transpose(1, 0, 2)[None], 0)
        return jnp.dot(
            spread.reshape(topk * count, experts * cut),
            b_factors[:, which].reshape(experts * cut, width),
            preferred_element_type=jnp.float32,
        ).reshape(topk, count, width)

    both = jnp.stack([base_gate + delta(0), base_up + delta(1)])
    both = lax.psum_scatter(both, "tok", scatter_dimension=3, tiled=True)
    scores = logit_here.astype(jnp.float32)
    first = jax.nn.sigmoid(scores[:, 0] - scores[:, 1])
    mixing = jnp.stack([first, 1.0 - first], axis=0)
    hidden = jnp.sum(mixing[:, :, None] * jax.nn.silu(both[0]) * both[1], axis=0)
    summed = jnp.dot(
        hidden.astype(jnp.bfloat16), down_weight, preferred_element_type=jnp.float32
    )
    return lax.psum_scatter(summed, BOTH, scatter_dimension=0, tiled=True).astype(jnp.bfloat16)


def solution(mesh):
    placed = (
        P(("parts", "fsdp", "tok"), None),
        P(("parts", "fsdp", "tok"), None),
        P(("parts", "fsdp", "tok"), None),
        P("tok", "fsdp"),
        P("tok", "fsdp"),
        P(("fsdp", "tok"), None),
        P(None, "fsdp", None),
        P(None, None, "tok", "fsdp"),
    )
    return jax.shard_map(
        fused_device if fits(mesh) else per_device,
        mesh=mesh,
        in_specs=placed,
        out_specs=P(("parts", "fsdp", "tok"), None),
        check_vma=False,
    )
```
